32 devices in a mesh: blk: 4 (over x, core), grp: 8 (over z, y).
Axes of the slice: x: 2, y: 2, z: 4, core: 2. Of those that a mesh axis runs over, the one named last changes fastest.
Arguments:
- amps: bfloat16 [1024, 2, 512], P(('blk', 'grp')), may hold values from -6 to 6
- domains: int32 [1024, 2], replicated, may hold values from 0 to 3, all different within a row
- owner: int32 [1024], replicated, may hold values from 0 to 1023, as said below
- coupling: int32 [4, 4], replicated, may hold values from 0 to 1, as said below
- integrals: bfloat16 [2048, 2048], P('blk', 'grp'), may hold values from -0.25 to 0.25
Outputs:
- residual: float32 [1024, 2048], P('blk', 'grp')
The draws below stay inside these ranges and needn't reach their ends.
Inputs may be any that keep to these rules, and one draw needn't show every extreme that they name: `domains`: each row names 2 different pair blocks, and every block is named by some row. owner maps the occupied pairs of each group of 256 consecutive pairs one to one onto the slots of the same group. Every column of coupling holds exactly 2 ones.
All inputs are finite; a program needn't handle non-finite values.
Results may differ from the reference program's by a relative error of at most 0.0003.
Values may be sent and summed in bfloat16 or wider, within the bound.
A program may use at most 64 MiB of HBM per device.

```python
import jax
import jax.numpy as jnp
from jax import lax

PB = 512
OP_GRP = 256
NVB = 4
NV = 2048
K = 2
OP = 1024


def draw_owner(key, part):
    n_groups = OP // OP_GRP
    group_keys = jax.random.split(key, n_groups)

    def shuffle_one(group_key):
        return jax.random.permutation(group_key, OP_GRP).astype(jnp.int32)
    shuffled = jax.vmap(shuffle_one)(group_keys)
    offsets = jnp.arange(n_groups, dtype=jnp.int32)[:, None] * OP_GRP
    return (shuffled + offsets).reshape(OP).astype(jnp.int32)


def draw_coupling(key, part):
    column_keys = jax.random.split(jax.random.fold_in(key, 7), NVB)

    def column_one(column_key):
        ranks = jax.random.permutation(column_key, NVB).astype(jnp.int32)
        return (ranks < NVB // 2).astype(jnp.int32)
    columns = jax.vmap(column_one)(column_keys)
    return jnp.transpose(columns).astype(jnp.int32)


def block_scale(own_key, shape, pieces, least, largest):
    def one(position, blocks):
        draws = jax.random.uniform(jax.random.fold_in(jax.random.fold_in(own_key, 6), position), (blocks,), jnp.float32, least / len(pieces), largest / len(pieces))
        return jnp.repeat(jnp.exp(draws), shape[position] // blocks).reshape((-1,) + (1,) * (len(shape) - position - 1))

    factor_of = one(*pieces[0])
    for cut in pieces[1:]:
        factor_of = factor_of * one(*cut)
    return factor_of


def picks_of(own_key, rows, amount, top, lift):
    sequence = jax.random.permutation(jax.random.fold_in(own_key, 1), amount)
    pull = sequence
    for power in range(3):
        pull = pull * pull // amount
    pull = pull * lift // amount
    tickets = jax.random.randint(jax.random.fold_in(own_key, 2), (rows, amount), 0, 4096) + pull
    fixed_rows = jax.random.permutation(jax.random.fold_in(own_key, 3), rows)[jnp.arange(amount) % rows]
    tickets = jnp.where(jnp.arange(rows)[:, None] == fixed_rows[None, :], 1 << 14, tickets)
    merit = tickets * amount + jnp.arange(amount)
    return lax.top_k(merit.astype(jnp.int32), top)[1].astype(jnp.int32)


def scatter_about(rng, shape, deviation, bound, shards=(), held_as=jnp.bfloat16):
    loudness = block_scale(rng, shape, shards, -0.22, 0.18) if shards else 1.0
    entries = jax.random.normal(rng, shape, jnp.float32) * deviation * loudness
    return jnp.minimum(jnp.maximum(entries, -bound), bound).astype(held_as)


def setup_inputs(seed: int = 0) -> dict:
    seeds = jax.random.split(jax.random.key(seed), 6)
    return {
        "amps": scatter_about(seeds[0], (OP, K, PB), 1.0, 6.0, ((0, 32),)),
        "domains": picks_of(seeds[1], OP, NVB, K, 4096),
        "owner": draw_owner(jax.random.fold_in(seeds[5], 71), 0),
        "coupling": draw_coupling(jax.random.fold_in(seeds[5], 71), 0),
        "integrals": scatter_about(seeds[4], (NV, NV), (K * PB // 2) ** -0.5, 0.25, ((0, 4), (1, 8))),
    }


def reference(amps, domains, owner, coupling, integrals):
    slot_dom = domains[owner]
    slot_amps = amps[owner]
    blocks = jnp.arange(NVB, dtype=jnp.int32)
    onehot = slot_dom[:, :, None] == blocks[None, None, :]
    tile_full = jnp.einsum("pkc,pkx->pcx", onehot.astype(jnp.float32), slot_amps.astype(jnp.float32))
    tile_full = tile_full.astype(jnp.bfloat16).reshape(OP, NV)
    in_domain = jnp.any(onehot, axis=1).astype(jnp.float32)

    def one_block(target):
        keep_mask = coupling[:, target].astype(jnp.bfloat16)
        masked = (tile_full.reshape(OP, NVB, PB) * keep_mask[None, :, None]).reshape(OP, NV)
        column_block = lax.dynamic_slice_in_dim(integrals, target * PB, PB, 1)
        return jnp.dot(masked, column_block, preferred_element_type=jnp.float32)

    by_block = lax.map(one_block, blocks)
    result = jnp.transpose(by_block, (1, 0, 2)) * in_domain[:, :, None]
    return result.reshape(OP, NV)
```

```python
import functools

import jax
import jax.numpy as jnp
from jax import lax
from jax.experimental import pallas as pl
from jax.experimental.pallas import tpu as pltpu
from jax.sharding import PartitionSpec as P

MESH = pl.DeviceIdType.MESH
F32 = jnp.float32
BF16 = jnp.bfloat16


def kernel(
    n_blk, n_grp, pieces,
    amps_ref, dom_ref, owner_ref, coupling_ref, ints_ref, out_ref,
    amp_buf, int_buf, tile_buf, code_buf,
    amp_z_send, amp_z_recv, amp_y_send, amp_y_recv,
    int_x_send, int_x_recv, int_c_send, int_c_recv, local_sem,
):
    chips, planes = n_blk // 2, n_grp // 2
    blk, grp = lax.axis_index("blk"), lax.axis_index("grp")
    x, core = blk // 2, blk % 2
    z, y = grp // 2, grp % 2
    slots, width, depth = amps_ref.shape
    rows = slots * width
    cols = ints_ref.shape[1]
    group = slots * n_grp
    nvb = n_blk
    target = grp // (depth // cols)
    cut = depth // pieces

    def at(b, g):
        return (b, g)

    mine = amp_buf.at[pl.ds(pl.multiple_of(grp * rows, rows), rows)]
    mine[...] = amps_ref[...].astype(F32).reshape(rows, depth).astype(BF16)

    peers = [at(blk, ((z + d) % planes) * 2 + y) for d in range(1, planes)]
    peers.append(at(blk, z * 2 + 1 - y))
    peers += [at(((x + d) % chips) * 2 + core, grp) for d in range(1, chips)]
    peers.append(at(x * 2 + 1 - core, grp))
    barrier = pltpu.get_barrier_semaphore()
    for peer in peers:
        pl.semaphore_signal(barrier, inc=1, device_id=peer, device_id_type=MESH)
    pl.semaphore_wait(barrier, len(peers))

    def amp_rows(g):
        return amp_buf.at[pl.ds(pl.multiple_of(g * rows, rows), rows)]

    def int_rows(b, p):
        return int_buf.at[b, pl.ds(p * cut, cut)]

    def amp_z(d):
        return pltpu.make_async_remote_copy(
            src_ref=amp_rows(grp), dst_ref=amp_rows(grp),
            send_sem=amp_z_send.at[d], recv_sem=amp_z_recv.at[d],
            device_id=at(blk, ((z + d) % planes) * 2 + y), device_id_type=MESH)

    def amp_y(d):
        g = ((z + planes - d) % planes) * 2 + y
        return pltpu.make_async_remote_copy(
            src_ref=amp_rows(g), dst_ref=amp_rows(g),
            send_sem=amp_y_send.at[d], recv_sem=amp_y_recv.at[d],
            device_id=at(blk, z * 2 + 1 - y), device_id_type=MESH)

    def int_x(d, p):
        return pltpu.make_async_remote_copy(
            src_ref=ints_ref.at[pl.ds(p * cut, cut)], dst_ref=int_rows(blk, p),
            send_sem=int_x_send.at[d, p], recv_sem=int_x_recv.at[d, p],
            device_id=at(((x + d) % chips) * 2 + core, grp), device_id_type=MESH)

    def int_c(d, p):
        b = ((x + chips - d) % chips) * 2 + core
        src = ints_ref.at[pl.ds(p * cut, cut)] if d == 0 else int_rows(b, p)
        return pltpu.make_async_remote_copy(
            src_ref=src, dst_ref=int_rows(b, p),
            send_sem=int_c_send.at[d, p], recv_sem=int_c_recv.at[d, p],
            device_id=at(x * 2 + 1 - core, grp), device_id_type=MESH)

    amp_y(0).start()
    for d in range(1, planes):
        amp_z(d).start()
    for p in range(pieces):
        for d in range(1, chips):
            int_x(d, p).start()
    for p in range(pieces):
        int_c(0, p).start()
    own_copy = pltpu.make_async_copy(ints_ref, int_buf.at[blk], local_sem)
    own_copy.start()

    dom = dom_ref[:, pl.ds(pl.multiple_of(blk * group, group), group)]
    own = owner_ref[:, pl.ds(pl.multiple_of(blk * group, group), group)] - blk * group
    hit = jnp.max((dom == target).astype(F32), axis=0, keepdims=True)
    keep = jnp.zeros(dom.shape, F32)
    for c in range(nvb):
        keep = jnp.where(dom == c, (coupling_ref[c, target] > 0).astype(F32), keep)
    code = keep * hit * (dom.astype(F32) + 1.0)
    j_slot = lax.broadcasted_iota(jnp.int32, (group, group * width), 1) // width
    spread = (j_slot == lax.broadcasted_iota(jnp.int32, (group, group * width), 0)).astype(F32)
    by_row = jnp.dot(code.astype(BF16), spread.astype(BF16), preferred_element_type=F32)
    j_k = lax.broadcasted_iota(jnp.int32, (width, group * width), 1) % width
    pick = j_k == lax.broadcasted_iota(jnp.int32, (width, group * width), 0)
    code_row = jnp.sum(jnp.where(pick, by_row, 0.0), axis=0, keepdims=True)
    diag = lax.broadcasted_iota(jnp.int32, (group, group), 0) == lax.broadcasted_iota(
        jnp.int32, (group, group), 1)
    own_col = jnp.sum(jnp.where(diag, own.astype(F32), 0.0), axis=1, keepdims=True)
    code_buf[...] = jnp.where(own_col == j_slot.astype(F32), code_row, 0.0)

    steps = max(planes, (chips - 1) * pieces + 1)
    arrivals = [(d, p) for p in range(pieces) for d in range(1, chips)]
    for s in range(1, steps):
        if s < planes:
            amp_z(s).wait_recv()
            amp_y(s).start()
        if s - 1 < len(arrivals) and s < planes:
            d, p = arrivals[s - 1]
            int_x(d, p).wait_recv()
            int_c(d, p).start()
    done = min(planes - 1, len(arrivals))
    for d in range(planes):
        amp_y(d).wait_recv()

    def build(c, _):
        sel = (code_buf[...] == (c + 1).astype(F32)).astype(F32).astype(BF16)
        tile_buf[c] = jnp.dot(sel, amp_buf[...], preferred_element_type=F32).astype(BF16)
        return 0

    if nvb <= 4:
        for c in range(nvb):
            build(jnp.int32(c), 0)
    else:
        lax.fori_loop(0, nvb, build, 0)

    own_copy.wait()
    out_ref[...] = jnp.dot(tile_buf[blk], int_buf[blk], preferred_element_type=F32)
    sib = x * 2 + 1 - core
    for p in range(pieces):
        int_c(0, p).wait_recv()
    out_ref[...] += jnp.dot(tile_buf[sib], int_buf[sib], preferred_element_type=F32)
    for d, p in arrivals[done:]:
        int_x(d, p).wait_recv()
        int_c(d, p).start()
    for p in range(pieces):
        for d in range(1, chips):
            b = ((x + chips - d) % chips) * 2
            span = pl.ds(p * cut, cut)
            part = jnp.dot(tile_buf[b + core, :, span], int_buf[b + core, span], preferred_element_type=F32)
            int_c(d, p).wait_recv()
            o = b + 1 - core
            part += jnp.dot(tile_buf[o, :, span], int_buf[o, span], preferred_element_type=F32)
            out_ref[...] += part

    for d in range(planes):
        amp_y(d).wait_send()
        if d > 0:
            amp_z(d).wait_send()
    for p in range(pieces):
        for d in range(chips):
            int_c(d, p).wait_send()
            if d > 0:
                int_x(d, p).wait_send()


def solution(mesh):
    n_blk, n_grp = mesh.shape["blk"], mesh.shape["grp"]

    def on_device(amps, domains, owner, coupling, integrals):
        slots, width, depth = amps.shape
        cols = integrals.shape[1]
        group = slots * n_grp
        pieces = 4
        chips, planes = n_blk // 2, n_grp // 2
        dma = pltpu.SemaphoreType.DMA
        vmem = pl.BlockSpec(memory_space=pltpu.VMEM)
        return pl.pallas_call(
            functools.partial(kernel, n_blk, n_grp, pieces),
            out_shape=jax.ShapeDtypeStruct((group, cols), F32),
            in_specs=[vmem, vmem, vmem, pl.BlockSpec(memory_space=pltpu.SMEM), pl.BlockSpec(memory_space=pl.ANY)],
            out_specs=vmem,
            scratch_shapes=[
                pltpu.VMEM((group * width, depth), BF16),
                pltpu.VMEM((n_blk, depth, cols), BF16),
                pltpu.VMEM((n_blk, group, depth), BF16),
                pltpu.VMEM((group, group * width), F32),
                dma((planes,)), dma((planes,)), dma((planes,)), dma((planes,)),
                dma((chips, pieces)), dma((chips, pieces)), dma((chips, pieces)), dma((chips, pieces)),
                dma(()),
            ],
            compiler_params=pltpu.CompilerParams(
                collective_id=0, has_side_effects=True, vmem_limit_bytes=40 * 1024 * 1024),
        )(amps, domains.T, owner.reshape(1, -1), coupling, integrals)

    return jax.shard_map(
        on_device,
        mesh=mesh,
        in_specs=(P(("blk", "grp"), None, None), P(), P(), P(), P("blk", "grp")),
        out_specs=P("blk", "grp"),
        check_vma=False,
    )
```

```python
import functools

import jax
import jax.numpy as jnp
from jax import lax
from jax.experimental import pallas as pl
from jax.experimental.pallas import tpu as pltpu
from jax.sharding import PartitionSpec as P

MESH = pl.DeviceIdType.MESH
F32 = jnp.float32
BF16 = jnp.bfloat16


def kernel(
    n_blk, n_grp, pieces,
    amps_hbm, dom_hbm, owner_hbm, coupling_hbm, ints_ref, out_ref,
    amps_ref, dom_ref, owner_ref, coupling_ref, load_sem, amp_buf, int_buf, tile_buf, code_buf,
    amp_z_send, amp_z_recv, amp_y_send, amp_y_recv,
    int_x_send, int_x_recv, int_c_send, int_c_recv, local_sem, ready,
):
    chips, planes = n_blk // 2, n_grp // 2
    blk, grp = lax.axis_index("blk"), lax.axis_index("grp")
    x, core = blk // 2, blk % 2
    z, y = grp // 2, grp % 2
    slots, width, depth = amps_ref.shape
    rows = slots * width
    cols = ints_ref.shape[1]
    group = slots * n_grp
    nvb = n_blk
    target = grp // (depth // cols)
    cut = depth // pieces

    def at(b, g):
        return (b, g)

    barrier = pltpu.get_barrier_semaphore()

    def greet(b, g):
        pl.semaphore_signal(barrier, inc=1, device_id=at(b, g), device_id_type=MESH)

    for d in range(1, chips):
        greet(((x + d) % chips) * 2 + core, grp)
    greet(x * 2 + 1 - core, grp)
    greet(blk, z * 2 + 1 - y)
    pl.when(z > 0)(lambda: greet(blk, grp - 2))
    pl.when(z < planes - 1)(lambda: greet(blk, grp + 2))

    loads = [
        pltpu.make_async_copy(src, dst, load_sem.at[i])
        for i, (src, dst) in enumerate((
            (amps_hbm, amps_ref), (dom_hbm, dom_ref), (owner_hbm, owner_ref), (coupling_hbm, coupling_ref)))
    ]
    for load in loads:
        load.start()
    own_copy = pltpu.make_async_copy(ints_ref, int_buf.at[blk], local_sem)
    own_copy.start()
    at_edge = jnp.where((z == 0) | (z == planes - 1), 1, 0)
    pl.semaphore_wait(barrier, chips + 3 - at_edge)

    def amp_rows(g):
        return amp_buf.at[pl.ds(pl.multiple_of(g * rows, rows), rows)]

    def int_rows(b, p):
        return int_buf.at[b, pl.ds(p * cut, cut)]

    def amp_z(src, dst):
        return pltpu.make_async_remote_copy(
            src_ref=amp_rows(src * 2 + y), dst_ref=amp_rows(src * 2 + y),
            send_sem=amp_z_send.at[dst], recv_sem=amp_z_recv.at[src],
            device_id=at(blk, dst * 2 + y), device_id_type=MESH)

    def amp_y(src):
        return pltpu.make_async_remote_copy(
            src_ref=amp_rows(src * 2 + y), dst_ref=amp_rows(src * 2 + y),
            send_sem=amp_y_send.at[src], recv_sem=amp_y_recv.at[src],
            device_id=at(blk, z * 2 + 1 - y), device_id_type=MESH)

    def both_sides(d, do):
        pl.when(z >= d)(lambda: do(z - d, 1))
        pl.when(z < planes - d)(lambda: do(z + d, -1))

    def int_x(d, p):
        return pltpu.make_async_remote_copy(
            src_ref=ints_ref.at[pl.ds(p * cut, cut)], dst_ref=int_rows(blk, p),
            send_sem=int_x_send.at[d, p], recv_sem=int_x_recv.at[d, p],
            device_id=at(((x + d) % chips) * 2 + core, grp), device_id_type=MESH)

    def int_c(d, p):
        b = ((x + chips - d) % chips) * 2 + core
        src = ints_ref.at[pl.ds(p * cut, cut)] if d == 0 else int_rows(b, p)
        return pltpu.make_async_remote_copy(
            src_ref=src, dst_ref=int_rows(b, p),
            send_sem=int_c_send.at[d, p], recv_sem=int_c_recv.at[d, p],
            device_id=at(x * 2 + 1 - core, grp), device_id_type=MESH)

    for p in range(pieces):
        for d in range(1, chips):
            int_x(d, p).start()
    loads[0].wait()
    amp_rows(grp)[...] = amps_ref[...].astype(F32).reshape(rows, depth).astype(BF16)
    both_sides(1, lambda to, _: amp_z(z, to).start())
    amp_y(z).start()

    def tell(other, step):
        def say():
            pl.semaphore_signal(ready.at[other], inc=1, device_id=at(blk, (z + step) * 2 + y), device_id_type=MESH)
        pl.when((z + step >= 0) & (z + step < planes))(say)

    def heard(other, step):
        pl.semaphore_wait(ready.at[other], 1)
        tell(other, step)
        amp_z(z, other).start()

    both_sides(1, tell)
    for d in range(2, planes):
        both_sides(d, heard)
    for p in range(pieces):
        int_c(0, p).start()

    for load in loads[1:]:
        load.wait()
    dom = dom_ref[:, pl.ds(pl.multiple_of(blk * group, group), group)]
    own = owner_ref[:, pl.ds(pl.multiple_of(blk * group, group), group)] - blk * group
    hit = jnp.max((dom == target).astype(F32), axis=0, keepdims=True)
    keep = jnp.zeros(dom.shape, F32)
    for c in range(nvb):
        keep = jnp.where(dom == c, (coupling_ref[c, target] > 0).astype(F32), keep)
    code = keep * hit * (dom.astype(F32) + 1.0)
    j_slot = lax.broadcasted_iota(jnp.int32, (group, group * width), 1) // width
    spread = (j_slot == lax.broadcasted_iota(jnp.int32, (group, group * width), 0)).astype(F32)
    by_row = jnp.dot(code.astype(BF16), spread.astype(BF16), preferred_element_type=F32)
    j_k = lax.broadcasted_iota(jnp.int32, (width, group * width), 1) % width
    pick = j_k == lax.broadcasted_iota(jnp.int32, (width, group * width), 0)
    code_row = jnp.sum(jnp.where(pick, by_row, 0.0), axis=0, keepdims=True)
    diag = lax.broadcasted_iota(jnp.int32, (group, group), 0) == lax.broadcasted_iota(
        jnp.int32, (group, group), 1)
    own_col = jnp.sum(jnp.where(diag, own.astype(F32), 0.0), axis=1, keepdims=True)
    code_buf[...] = jnp.where(own_col == j_slot.astype(F32), code_row, 0.0)

    arrivals = [(d, p) for p in range(pieces) for d in range(1, chips)]

    def pass_int(some):
        for d, p in some:
            int_x(d, p).wait_recv()
            int_c(d, p).start()

    def pass_amp(src, _):
        amp_z(src, z).wait_recv()
        amp_y(src).start()

    share = len(arrivals) // (2 * planes)
    for d in range(1, planes):
        both_sides(d, pass_amp)
        pass_int(arrivals[(d - 1) * share:d * share])
    done = (planes - 1) * share
    for src in range(planes):
        amp_y(src).wait_recv()

    def build(c, _):
        sel = (code_buf[...] == (c + 1).astype(F32)).astype(F32).astype(BF16)
        tile_buf[c] = jnp.dot(sel, amp_buf[...], preferred_element_type=F32).astype(BF16)
        return 0

    if nvb <= 4:
        for c in range(nvb):
            build(jnp.int32(c), 0)
    else:
        lax.fori_loop(0, nvb, build, 0)

    own_copy.wait()
    out_ref[...] = jnp.dot(tile_buf[blk], int_buf[blk], preferred_element_type=F32)
    sib = x * 2 + 1 - core
    for p in range(pieces):
        int_c(0, p).wait_recv()
    out_ref[...] += jnp.dot(tile_buf[sib], int_buf[sib], preferred_element_type=F32)
    pass_int(arrivals[done:])
    for p in range(pieces):
        for d in range(1, chips):
            b = ((x + chips - d) % chips) * 2
            span = pl.ds(p * cut, cut)
            part = jnp.dot(tile_buf[b + core, :, span], int_buf[b + core, span], preferred_element_type=F32)
            int_c(d, p).wait_recv()
            o = b + 1 - core
            part += jnp.dot(tile_buf[o, :, span], int_buf[o, span], preferred_element_type=F32)
            out_ref[...] += part

    for d in range(planes):
        amp_y(d).wait_send()
        if d > 0:
            both_sides(d, lambda to, _: amp_z(z, to).wait_send())
    for p in range(pieces):
        for d in range(chips):
            int_c(d, p).wait_send()
            if d > 0:
                int_x(d, p).wait_send()


def solution(mesh):
    n_blk, n_grp = mesh.shape["blk"], mesh.shape["grp"]

    def on_device(amps, domains, owner, coupling, integrals):
        slots, width, depth = amps.shape
        cols = integrals.shape[1]
        group = slots * n_grp
        pieces = 8
        chips, planes = n_blk // 2, n_grp // 2
        dma = pltpu.SemaphoreType.DMA
        vmem = pl.BlockSpec(memory_space=pltpu.VMEM)
        return pl.pallas_call(
            functools.partial(kernel, n_blk, n_grp, pieces),
            out_shape=jax.ShapeDtypeStruct((group, cols), F32),
            in_specs=[pl.BlockSpec(memory_space=pltpu.HBM)] * 5,
            out_specs=vmem,
            scratch_shapes=[
                pltpu.VMEM(amps.shape, BF16),
                pltpu.VMEM((width, domains.shape[0]), jnp.int32),
                pltpu.VMEM((1, owner.shape[0]), jnp.int32),
                pltpu.SMEM(coupling.shape, jnp.int32),
                dma((4,)),
                pltpu.VMEM((group * width, depth), BF16),
                pltpu.VMEM((n_blk, depth, cols), BF16),
                pltpu.VMEM((n_blk, group, depth), BF16),
                pltpu.VMEM((group, group * width), F32),
                dma((planes,)), dma((planes,)), dma((planes,)), dma((planes,)),
                dma((chips, pieces)), dma((chips, pieces)), dma((chips, pieces)), dma((chips, pieces)),
                dma(()), pltpu.SemaphoreType.REGULAR((planes,)),
            ],
            compiler_params=pltpu.CompilerParams(
                collective_id=0, has_side_effects=True, vmem_limit_bytes=48 * 1024 * 1024),
        )(*(pltpu.with_memory_space_constraint(a, pltpu.HBM) for a in (amps, domains.T, owner.reshape(1, -1), coupling, integrals)))

    return jax.shard_map(
        on_device,
        mesh=mesh,
        in_specs=(P(("blk", "grp"), None, None), P(), P(), P(), P("blk", "grp")),
        out_specs=P("blk", "grp"),
        check_vma=False,
    )
```

```python
import functools

import jax
import jax.numpy as jnp
from jax import lax
from jax.experimental import pallas as pl
from jax.experimental.pallas import tpu as pltpu
from jax.sharding import PartitionSpec as P

MESH = pl.DeviceIdType.MESH
F32 = jnp.float32
BF16 = jnp.bfloat16


def kernel(
    n_blk, n_grp, pieces, late,
    amps_hbm, dom_hbm, owner_hbm, coupling_hbm, ints_ref, out_ref,
    amps_ref, dom_ref, owner_ref, coupling_ref, load_sem, amp_buf, int_buf, tile_buf, code_buf,
    whole_send, whole_recv, other_send, other_recv, cross_send, cross_recv, late_send, late_recv,
    int_x_send, int_x_recv, int_c_send, int_c_recv, local_sem,
):
    chips, planes = n_blk // 2, n_grp // 2
    blk, grp = lax.axis_index("blk"), lax.axis_index("grp")
    x, core = blk // 2, blk % 2
    z, y = grp // 2, grp % 2
    slots, width, depth = amps_ref.shape
    rows = slots * width
    cols = ints_ref.shape[1]
    group = slots * n_grp
    nvb = n_blk
    target = grp // (depth // cols)
    cut = depth // pieces

    def at(b, g):
        return (b, g)

    barrier = pltpu.get_barrier_semaphore()

    def greet(b, g):
        pl.semaphore_signal(barrier, inc=1, device_id=at(b, g), device_id_type=MESH)

    for d in range(1, chips):
        greet(((x + d) % chips) * 2 + core, grp)
    greet(x * 2 + 1 - core, grp)
    greet(blk, z * 2 + 1 - y)
    pl.when(z > 0)(lambda: greet(blk, grp - 2))
    pl.when(z < planes - 1)(lambda: greet(blk, grp + 2))

    loads = [
        pltpu.make_async_copy(src, dst, load_sem.at[i])
        for i, (src, dst) in enumerate((
            (amps_hbm, amps_ref), (dom_hbm, dom_ref), (owner_hbm, owner_ref), (coupling_hbm, coupling_ref)))
    ]
    for load in loads:
        load.start()
    own_copy = pltpu.make_async_copy(ints_ref, int_buf.at[blk], local_sem)
    own_copy.start()
    at_edge = jnp.where((z == 0) | (z == planes - 1), 1, 0)
    pl.semaphore_wait(barrier, chips + 3 - at_edge)

    def amp_rows(g):
        return amp_buf.at[pl.ds(pl.multiple_of(g * rows, rows), rows)]

    def int_rows(b, p):
        return int_buf.at[b, pl.ds(p * cut, cut)]

    early = rows - late

    def copy(g, first, count, send, recv, to):
        where = amp_buf.at[pl.ds(pl.multiple_of(g * rows + first, 16), count)]
        return pltpu.make_async_remote_copy(
            src_ref=where, dst_ref=where, send_sem=send, recv_sem=recv, device_id=to, device_id_type=MESH)

    def whole(src, step, s=None):
        sem = src if s is None else s
        return copy(src * 2 + y, 0, rows, whole_send.at[sem], whole_recv.at[src], at(blk, grp + 2 * step))

    def other(src, step, s=None):
        sem = src if s is None else s
        return copy(src * 2 + 1 - y, early, late, other_send.at[sem], other_recv.at[src], at(blk, grp + 2 * step))

    def cross(src):
        return copy(src * 2 + y, 0, early, cross_send.at[src], cross_recv.at[src], at(blk, z * 2 + 1 - y))

    def cross_late(g):
        return copy(g, early, late, late_send, late_recv, at(blk, z * 2 + 1 - y))

    def up(do):
        pl.when(z < planes - 1)(do)

    def down(do):
        pl.when(z > 0)(do)

    def both_sides(d, do):
        pl.when(z >= d)(lambda: do(z - d, 1))
        pl.when(z < planes - d)(lambda: do(z + d, -1))

    def int_x(d, p):
        return pltpu.make_async_remote_copy(
            src_ref=ints_ref.at[pl.ds(p * cut, cut)], dst_ref=int_rows(blk, p),
            send_sem=int_x_send.at[d, p], recv_sem=int_x_recv.at[d, p],
            device_id=at(((x + d) % chips) * 2 + core, grp), device_id_type=MESH)

    def int_c(d, p):
        b = ((x + chips - d) % chips) * 2 + core
        src = ints_ref.at[pl.ds(p * cut, cut)] if d == 0 else int_rows(b, p)
        return pltpu.make_async_remote_copy(
            src_ref=src, dst_ref=int_rows(b, p),
            send_sem=int_c_send.at[d, p], recv_sem=int_c_recv.at[d, p],
            device_id=at(x * 2 + 1 - core, grp), device_id_type=MESH)

    for p in range(pieces):
        for d in range(1, chips):
            int_x(d, p).start()
    loads[0].wait()
    amp_rows(grp)[...] = amps_ref[...].astype(F32).reshape(rows, depth).astype(BF16)
    cross_late(grp).start()
    up(lambda: whole(z, 1).start())
    down(lambda: whole(z, -1, planes).start())
    cross(z).start()
    for p in range(pieces):
        int_c(0, p).start()
    cross_late(z * 2 + 1 - y).wait_recv()
    up(lambda: other(z, 1).start())
    down(lambda: other(z, -1, planes).start())

    for load in loads[1:]:
        load.wait()
    dom = dom_ref[:, pl.ds(pl.multiple_of(blk * group, group), group)]
    own = owner_ref[:, pl.ds(pl.multiple_of(blk * group, group), group)] - blk * group
    hit = jnp.max((dom == target).astype(F32), axis=0, keepdims=True)
    keep = jnp.zeros(dom.shape, F32)
    kept = nvb // 2
    rank = jnp.int32(0)
    block_of = [jnp.int32(0)] * kept
    for c in range(nvb):
        on = (coupling_ref[c, target] > 0).astype(jnp.int32)
        for r in range(kept):
            block_of[r] += jnp.where((on > 0) & (rank == r), c, 0)
        rank += on
        keep = jnp.where(dom == c, (on * rank).astype(F32), keep)
    code = keep * hit
    j_slot = lax.broadcasted_iota(jnp.int32, (group, group * width), 1) // width
    spread = (j_slot == lax.broadcasted_iota(jnp.int32, (group, group * width), 0)).astype(F32)
    by_row = jnp.dot(code.astype(BF16), spread.astype(BF16), preferred_element_type=F32)
    j_k = lax.broadcasted_iota(jnp.int32, (width, group * width), 1) % width
    pick = j_k == lax.broadcasted_iota(jnp.int32, (width, group * width), 0)
    code_row = jnp.sum(jnp.where(pick, by_row, 0.0), axis=0, keepdims=True)
    diag = lax.broadcasted_iota(jnp.int32, (group, group), 0) == lax.broadcasted_iota(
        jnp.int32, (group, group), 1)
    own_col = jnp.sum(jnp.where(diag, own.astype(F32), 0.0), axis=1, keepdims=True)
    code_buf[...] = jnp.where(own_col == j_slot.astype(F32), code_row, 0.0)

    arrivals = [(d, p) for p in range(pieces) for d in range(1, chips)]

    def pass_int(some):
        for d, p in some:
            int_x(d, p).wait_recv()
            int_c(d, p).start()

    def pass_amp(src, step):
        further = (z + step >= 0) & (z + step < planes)
        whole(src, step).wait_recv()
        pl.when(further)(lambda: whole(src, step).start())
        cross(src).start()
        other(src, step).wait_recv()
        pl.when(further)(lambda: other(src, step).start())

    share = len(arrivals) // (2 * planes)
    for d in range(1, planes):
        both_sides(d, pass_amp)
        pass_int(arrivals[(d - 1) * share:d * share])
    done = (planes - 1) * share
    for src in range(planes):
        cross(src).wait_recv()

    def build(c, _):
        sel = (code_buf[...] == (c + 1).astype(F32)).astype(F32).astype(BF16)
        tile_buf[c] = jnp.dot(sel, amp_buf[...], preferred_element_type=F32).astype(BF16)
        return 0

    pass_int(arrivals[done:])
    if kept <= 4:
        for r in range(kept):
            build(jnp.int32(r), 0)
    else:
        lax.fori_loop(0, kept, build, 0)

    own_copy.wait()
    for p in range(pieces):
        for d in range(chips):
            int_c(d, p).wait_recv()
    total = jnp.dot(tile_buf[0], int_buf[block_of[0]], preferred_element_type=F32)
    for r in range(1, kept):
        total += jnp.dot(tile_buf[r], int_buf[block_of[r]], preferred_element_type=F32)
    out_ref[...] = total

    def sent(src, step):
        further = (z + step >= 0) & (z + step < planes)
        pl.when(further)(lambda: whole(src, step).wait_send())
        pl.when(further)(lambda: other(src, step).wait_send())

    cross_late(grp).wait_send()
    for src in range(planes):
        cross(src).wait_send()
    up(lambda: whole(z, 1).wait_send())
    up(lambda: other(z, 1).wait_send())
    down(lambda: whole(z, -1, planes).wait_send())
    down(lambda: other(z, -1, planes).wait_send())
    for d in range(1, planes):
        both_sides(d, sent)
    for p in range(pieces):
        for d in range(chips):
            int_c(d, p).wait_send()
            if d > 0:
                int_x(d, p).wait_send()


def solution(mesh):
    n_blk, n_grp = mesh.shape["blk"], mesh.shape["grp"]

    def on_device(amps, domains, owner, coupling, integrals):
        slots, width, depth = amps.shape
        cols = integrals.shape[1]
        group = slots * n_grp
        pieces = 4
        late = slots * width // 2
        chips, planes = n_blk // 2, n_grp // 2
        dma = pltpu.SemaphoreType.DMA
        vmem = pl.BlockSpec(memory_space=pltpu.VMEM)
        return pl.pallas_call(
            functools.partial(kernel, n_blk, n_grp, pieces, late),
            out_shape=jax.ShapeDtypeStruct((group, cols), F32),
            in_specs=[pl.BlockSpec(memory_space=pltpu.HBM)] * 5,
            out_specs=vmem,
            scratch_shapes=[
                pltpu.VMEM(amps.shape, BF16),
                pltpu.VMEM((width, domains.shape[0]), jnp.int32),
                pltpu.VMEM((1, owner.shape[0]), jnp.int32),
                pltpu.SMEM(coupling.shape, jnp.int32),
                dma((4,)),
                pltpu.VMEM((group * width, depth), BF16),
                pltpu.VMEM((n_blk, depth, cols), BF16),
                pltpu.VMEM((n_blk // 2, group, depth), BF16),
                pltpu.VMEM((group, group * width), F32),
                dma((planes + 1,)), dma((planes,)), dma((planes + 1,)), dma((planes,)),
                dma((planes,)), dma((planes,)), dma(()), dma(()),
                dma((chips, pieces)), dma((chips, pieces)), dma((chips, pieces)), dma((chips, pieces)),
                dma(()),
            ],
            compiler_params=pltpu.CompilerParams(
                collective_id=0, has_side_effects=True, vmem_limit_bytes=48 * 1024 * 1024),
        )(*(pltpu.with_memory_space_constraint(a, pltpu.HBM) for a in (amps, domains.T, owner.reshape(1, -1), coupling, integrals)))

    return jax.shard_map(
        on_device,
        mesh=mesh,
        in_specs=(P(("blk", "grp"), None, None), P(), P(), P(), P("blk", "grp")),
        out_specs=P("blk", "grp"),
        check_vma=False,
    )
```

```python
import functools

import jax
import jax.numpy as jnp
from jax import lax
from jax.experimental import pallas as pl
from jax.experimental.pallas import tpu as pltpu
from jax.sharding import PartitionSpec as P

MESH = pl.DeviceIdType.MESH
F32 = jnp.float32
BF16 = jnp.bfloat16


def kernel(
    n_blk, n_grp, pieces,
    amps_hbm, dom_hbm, owner_hbm, coupling_hbm, ints_ref, out_ref,
    amps_ref, dom_ref, owner_ref, coupling_ref, load_sem, amp_buf, int_buf, tile_buf, code_buf,
    amp_z_send, amp_z_recv, amp_y_send, amp_y_recv,
    int_x_send, int_x_recv, int_c_send, int_c_recv, local_sem, ready,
):
    chips, planes = n_blk // 2, n_grp // 2
    blk, grp = lax.axis_index("blk"), lax.axis_index("grp")
    x, core = blk // 2, blk % 2
    z, y = grp // 2, grp % 2
    slots, width, depth = amps_ref.shape
    rows = slots * width
    cols = ints_ref.shape[1]
    group = slots * n_grp
    nvb = n_blk
    target = grp // (depth // cols)
    cut = depth // pieces

    def at(b, g):
        return (b, g)

    barrier = pltpu.get_barrier_semaphore()

    def greet(b, g):
        pl.semaphore_signal(barrier, inc=1, device_id=at(b, g), device_id_type=MESH)

    for d in range(1, chips):
        greet(((x + d) % chips) * 2 + core, grp)
    greet(x * 2 + 1 - core, grp)
    greet(blk, z * 2 + 1 - y)
    pl.when(z > 0)(lambda: greet(blk, grp - 2))
    pl.when(z < planes - 1)(lambda: greet(blk, grp + 2))

    loads = [
        pltpu.make_async_copy(src, dst, load_sem.at[i])
        for i, (src, dst) in enumerate((
            (amps_hbm, amps_ref), (dom_hbm, dom_ref), (owner_hbm, owner_ref), (coupling_hbm, coupling_ref)))
    ]
    for load in loads:
        load.start()
    own_copy = pltpu.make_async_copy(ints_ref, int_buf.at[blk], local_sem)
    own_copy.start()
    at_edge = jnp.where((z == 0) | (z == planes - 1), 1, 0)
    pl.semaphore_wait(barrier, chips + 3 - at_edge)

    def amp_rows(g):
        return amp_buf.at[pl.ds(pl.multiple_of(g * rows, rows), rows)]

    def int_rows(b, p):
        return int_buf.at[b, pl.ds(p * cut, cut)]

    def amp_z(src, dst):
        return pltpu.make_async_remote_copy(
            src_ref=amp_rows(src * 2 + y), dst_ref=amp_rows(src * 2 + y),
            send_sem=amp_z_send.at[dst], recv_sem=amp_z_recv.at[src],
            device_id=at(blk, dst * 2 + y), device_id_type=MESH)

    def amp_y(src):
        return pltpu.make_async_remote_copy(
            src_ref=amp_rows(src * 2 + y), dst_ref=amp_rows(src * 2 + y),
            send_sem=amp_y_send.at[src], recv_sem=amp_y_recv.at[src],
            device_id=at(blk, z * 2 + 1 - y), device_id_type=MESH)

    def both_sides(d, do):
        pl.when(z >= d)(lambda: do(z - d, 1))
        pl.when(z < planes - d)(lambda: do(z + d, -1))

    def int_x(d, p):
        return pltpu.make_async_remote_copy(
            src_ref=ints_ref.at[pl.ds(p * cut, cut)], dst_ref=int_rows(blk, p),
            send_sem=int_x_send.at[d, p], recv_sem=int_x_recv.at[d, p],
            device_id=at(((x + d) % chips) * 2 + core, grp), device_id_type=MESH)

    def int_c(d, p):
        b = ((x + chips - d) % chips) * 2 + core
        src = ints_ref.at[pl.ds(p * cut, cut)] if d == 0 else int_rows(b, p)
        return pltpu.make_async_remote_copy(
            src_ref=src, dst_ref=int_rows(b, p),
            send_sem=int_c_send.at[d, p], recv_sem=int_c_recv.at[d, p],
            device_id=at(x * 2 + 1 - core, grp), device_id_type=MESH)

    for p in range(pieces):
        for d in range(1, chips):
            int_x(d, p).start()
    loads[0].wait()
    amp_rows(grp)[...] = amps_ref[...].astype(F32).reshape(rows, depth).astype(BF16)
    both_sides(1, lambda to, _: amp_z(z, to).start())
    amp_y(z).start()

    def tell(other, step):
        def say():
            pl.semaphore_signal(ready.at[other], inc=1, device_id=at(blk, (z + step) * 2 + y), device_id_type=MESH)
        pl.when((z + step >= 0) & (z + step < planes))(say)

    def heard(other, step):
        pl.semaphore_wait(ready.at[other], 1)
        tell(other, step)
        amp_z(z, other).start()

    both_sides(1, tell)
    for d in range(2, planes):
        both_sides(d, heard)
    for p in range(pieces):
        int_c(0, p).start()

    for load in loads[1:]:
        load.wait()
    dom = dom_ref[:, pl.ds(pl.multiple_of(blk * group, group), group)]
    own = owner_ref[:, pl.ds(pl.multiple_of(blk * group, group), group)] - blk * group
    hit = jnp.max((dom == target).astype(F32), axis=0, keepdims=True)
    keep = jnp.zeros(dom.shape, F32)
    kept = nvb // 2
    rank = jnp.int32(0)
    block_of = [jnp.int32(0)] * kept
    for c in range(nvb):
        on = (coupling_ref[c, target] > 0).astype(jnp.int32)
        for r in range(kept):
            block_of[r] += jnp.where((on > 0) & (rank == r), c, 0)
        rank += on
        keep = jnp.where(dom == c, (on * rank).astype(F32), keep)
    code = keep * hit
    j_slot = lax.broadcasted_iota(jnp.int32, (group, group * width), 1) // width
    spread = (j_slot == lax.broadcasted_iota(jnp.int32, (group, group * width), 0)).astype(F32)
    by_row = jnp.dot(code.astype(BF16), spread.astype(BF16), preferred_element_type=F32)
    j_k = lax.broadcasted_iota(jnp.int32, (width, group * width), 1) % width
    pick = j_k == lax.broadcasted_iota(jnp.int32, (width, group * width), 0)
    code_row = jnp.sum(jnp.where(pick, by_row, 0.0), axis=0, keepdims=True)
    diag = lax.broadcasted_iota(jnp.int32, (group, group), 0) == lax.broadcasted_iota(
        jnp.int32, (group, group), 1)
    own_col = jnp.sum(jnp.where(diag, own.astype(F32), 0.0), axis=1, keepdims=True)
    code_buf[...] = jnp.where(own_col == j_slot.astype(F32), code_row, 0.0)

    arrivals = [(d, p) for p in range(pieces) for d in range(1, chips)]

    def pass_int(some):
        for d, p in some:
            int_x(d, p).wait_recv()
            int_c(d, p).start()

    def pass_amp(src, _):
        amp_z(src, z).wait_recv()
        amp_y(src).start()

    for d in range(1, planes):
        both_sides(d, pass_amp)
    pass_int(arrivals)
    for src in range(planes):
        amp_y(src).wait_recv()

    def build(c, _):
        sel = (code_buf[...] == (c + 1).astype(F32)).astype(F32).astype(BF16)
        tile_buf[c] = jnp.dot(sel, amp_buf[...], preferred_element_type=F32).astype(BF16)
        return 0

    if kept <= 4:
        for r in range(kept):
            build(jnp.int32(r), 0)
    else:
        lax.fori_loop(0, kept, build, 0)

    own_copy.wait()
    for p in range(pieces):
        for d in range(chips):
            int_c(d, p).wait_recv()
    total = jnp.dot(tile_buf[0], int_buf[block_of[0]], preferred_element_type=F32)
    for r in range(1, kept):
        total += jnp.dot(tile_buf[r], int_buf[block_of[r]], preferred_element_type=F32)
    out_ref[...] = total

    for d in range(planes):
        amp_y(d).wait_send()
        if d > 0:
            both_sides(d, lambda to, _: amp_z(z, to).wait_send())
    for p in range(pieces):
        for d in range(chips):
            int_c(d, p).wait_send()
            if d > 0:
                int_x(d, p).wait_send()


def solution(mesh):
    n_blk, n_grp = mesh.shape["blk"], mesh.shape["grp"]

    def on_device(amps, domains, owner, coupling, integrals):
        slots, width, depth = amps.shape
        cols = integrals.shape[1]
        group = slots * n_grp
        pieces = 4
        chips, planes = n_blk // 2, n_grp // 2
        dma = pltpu.SemaphoreType.DMA
        vmem = pl.BlockSpec(memory_space=pltpu.VMEM)
        return pl.pallas_call(
            functools.partial(kernel, n_blk, n_grp, pieces),
            out_shape=jax.ShapeDtypeStruct((group, cols), F32),
            in_specs=[pl.BlockSpec(memory_space=pltpu.HBM)] * 5,
            out_specs=vmem,
            scratch_shapes=[
                pltpu.VMEM(amps.shape, BF16),
                pltpu.VMEM((width, domains.shape[0]), jnp.int32),
                pltpu.VMEM((1, owner.shape[0]), jnp.int32),
                pltpu.SMEM(coupling.shape, jnp.int32),
                dma((4,)),
                pltpu.VMEM((group * width, depth), BF16),
                pltpu.VMEM((n_blk, depth, cols), BF16),
                pltpu.VMEM((n_blk // 2, group, depth), BF16),
                pltpu.VMEM((group, group * width), F32),
                dma((planes,)), dma((planes,)), dma((planes,)), dma((planes,)),
                dma((chips, pieces)), dma((chips, pieces)), dma((chips, pieces)), dma((chips, pieces)),
                dma(()), pltpu.SemaphoreType.REGULAR((planes,)),
            ],
            compiler_params=pltpu.CompilerParams(
                collective_id=0, has_side_effects=True, vmem_limit_bytes=48 * 1024 * 1024),
        )(*(pltpu.with_memory_space_constraint(a, pltpu.HBM) for a in (amps, domains.T, owner.reshape(1, -1), coupling, integrals)))

    return jax.shard_map(
        on_device,
        mesh=mesh,
        in_specs=(P(("blk", "grp"), None, None), P(), P(), P(), P("blk", "grp")),
        out_specs=P("blk", "grp"),
        check_vma=False,
    )
```

```python
import functools

import jax
import jax.numpy as jnp
from jax import lax
from jax.experimental import pallas as pl
from jax.experimental.pallas import tpu as pltpu
from jax.sharding import PartitionSpec as P

MESH = pl.DeviceIdType.MESH
F32 = jnp.float32
BF16 = jnp.bfloat16


def kernel(
    n_blk, n_grp, pieces,
    amps_hbm, dom_hbm, owner_hbm, coupling_hbm, ints_ref, out_ref,
    amps_ref, dom_ref, owner_ref, coupling_ref, load_sem, amp_buf, int_buf, tile_buf, code_buf,
    amp_z_send, amp_z_recv, amp_y_send, amp_y_recv,
    int_x_send, int_x_recv, int_c_send, int_c_recv, local_sem, ready,
):
    chips, planes = n_blk // 2, n_grp // 2
    blk, grp = lax.axis_index("blk"), lax.axis_index("grp")
    x, core = blk // 2, blk % 2
    z, y = grp // 2, grp % 2
    slots, width, depth = amps_ref.shape
    rows = slots * width
    cols = ints_ref.shape[1]
    group = slots * n_grp
    nvb = n_blk
    target = grp // (depth // cols)
    cut = depth // pieces

    def at(b, g):
        return (b, g)

    barrier = pltpu.get_barrier_semaphore()

    def greet(b, g):
        pl.semaphore_signal(barrier, inc=1, device_id=at(b, g), device_id_type=MESH)

    for d in range(1, chips):
        greet(((x + d) % chips) * 2 + core, grp)
    greet(x * 2 + 1 - core, grp)
    greet(blk, z * 2 + 1 - y)
    pl.when(z > 0)(lambda: greet(blk, grp - 2))
    pl.when(z < planes - 1)(lambda: greet(blk, grp + 2))

    loads = [
        pltpu.make_async_copy(src, dst, load_sem.at[i])
        for i, (src, dst) in enumerate((
            (amps_hbm, amps_ref), (dom_hbm, dom_ref), (owner_hbm, owner_ref), (coupling_hbm, coupling_ref)))
    ]
    for load in loads:
        load.start()
    own_copy = pltpu.make_async_copy(ints_ref, int_buf.at[blk], local_sem)
    own_copy.start()
    at_edge = jnp.where((z == 0) | (z == planes - 1), 1, 0)
    pl.semaphore_wait(barrier, chips + 3 - at_edge)

    def amp_rows(g):
        return amp_buf.at[pl.ds(pl.multiple_of(g * rows, rows), rows)]

    def int_rows(b, p):
        return int_buf.at[b, pl.ds(p * cut, cut)]

    def amp_z(src, dst):
        return pltpu.make_async_remote_copy(
            src_ref=amp_rows(src * 2 + y), dst_ref=amp_rows(src * 2 + y),
            send_sem=amp_z_send.at[dst], recv_sem=amp_z_recv.at[src],
            device_id=at(blk, dst * 2 + y), device_id_type=MESH)

    def amp_y(src):
        return pltpu.make_async_remote_copy(
            src_ref=amp_rows(src * 2 + y), dst_ref=amp_rows(src * 2 + y),
            send_sem=amp_y_send.at[src], recv_sem=amp_y_recv.at[src],
            device_id=at(blk, z * 2 + 1 - y), device_id_type=MESH)

    def both_sides(d, do):
        pl.when(z >= d)(lambda: do(z - d, 1))
        pl.when(z < planes - d)(lambda: do(z + d, -1))

    def int_x(d, p):
        return pltpu.make_async_remote_copy(
            src_ref=ints_ref.at[pl.ds(p * cut, cut)], dst_ref=int_rows(blk, p),
            send_sem=int_x_send.at[d, p], recv_sem=int_x_recv.at[d, p],
            device_id=at(((x + d) % chips) * 2 + core, grp), device_id_type=MESH)

    def int_c(d, p):
        b = ((x + chips - d) % chips) * 2 + core
        src = ints_ref.at[pl.ds(p * cut, cut)] if d == 0 else int_rows(b, p)
        return pltpu.make_async_remote_copy(
            src_ref=src, dst_ref=int_rows(b, p),
            send_sem=int_c_send.at[d, p], recv_sem=int_c_recv.at[d, p],
            device_id=at(x * 2 + 1 - core, grp), device_id_type=MESH)

    for p in range(pieces):
        for d in range(1, chips):
            int_x(d, p).start()
    def tell(other, step):
        def say():
            pl.semaphore_signal(ready.at[other], inc=1, device_id=at(blk, (z + step) * 2 + y), device_id_type=MESH)
        pl.when((z + step >= 0) & (z + step < planes))(say)

    def heard(other, step):
        pl.semaphore_wait(ready.at[other], 1)
        tell(other, step)
        amp_z(z, other).start()

    both_sides(1, tell)
    loads[0].wait()
    amp_rows(grp)[...] = amps_ref[...].astype(F32).reshape(rows, depth).astype(BF16)
    both_sides(1, lambda to, _: amp_z(z, to).start())
    amp_y(z).start()

    for p in range(pieces):
        int_c(0, p).start()

    for load in loads[1:]:
        load.wait()
    dom = dom_ref[:, pl.ds(pl.multiple_of(blk * group, group), group)]
    own = owner_ref[:, pl.ds(pl.multiple_of(blk * group, group), group)] - blk * group
    hit = jnp.max((dom == target).astype(F32), axis=0, keepdims=True)
    keep = jnp.zeros(dom.shape, F32)
    kept = nvb // 2
    rank = jnp.int32(0)
    block_of = [jnp.int32(0)] * kept
    for c in range(nvb):
        on = (coupling_ref[c, target] > 0).astype(jnp.int32)
        for r in range(kept):
            block_of[r] += jnp.where((on > 0) & (rank == r), c, 0)
        rank += on
        keep = jnp.where(dom == c, (on * rank).astype(F32), keep)
    code = keep * hit
    j_slot = lax.broadcasted_iota(jnp.int32, (group, group * width), 1) // width
    spread = (j_slot == lax.broadcasted_iota(jnp.int32, (group, group * width), 0)).astype(F32)
    by_row = jnp.dot(code.astype(BF16), spread.astype(BF16), preferred_element_type=F32)
    j_k = lax.broadcasted_iota(jnp.int32, (width, group * width), 1) % width
    pick = j_k == lax.broadcasted_iota(jnp.int32, (width, group * width), 0)
    code_row = jnp.sum(jnp.where(pick, by_row, 0.0), axis=0, keepdims=True)
    diag = lax.broadcasted_iota(jnp.int32, (group, group), 0) == lax.broadcasted_iota(
        jnp.int32, (group, group), 1)
    own_col = jnp.sum(jnp.where(diag, own.astype(F32), 0.0), axis=1, keepdims=True)
    code_buf[...] = jnp.where(own_col == j_slot.astype(F32), code_row, 0.0)

    arrivals = [(d, p) for p in range(pieces) for d in range(1, chips)]

    def pass_int(some):
        for d, p in some:
            int_x(d, p).wait_recv()
            int_c(d, p).start()

    def pass_amp(src, _):
        amp_z(src, z).wait_recv()
        amp_y(src).start()

    for d in range(2, planes):
        both_sides(d, heard)
        both_sides(d - 1, pass_amp)
    both_sides(planes - 1, pass_amp)
    pass_int(arrivals)
    for src in range(planes):
        amp_y(src).wait_recv()

    def build(c, _):
        sel = (code_buf[...] == (c + 1).astype(F32)).astype(F32).astype(BF16)
        tile_buf[c] = jnp.dot(sel, amp_buf[...], preferred_element_type=F32).astype(BF16)
        return 0

    if kept <= 4:
        for r in range(kept):
            build(jnp.int32(r), 0)
    else:
        lax.fori_loop(0, kept, build, 0)

    own_copy.wait()
    for p in range(pieces):
        for d in range(chips):
            int_c(d, p).wait_recv()
    total = jnp.dot(tile_buf[0], int_buf[block_of[0]], preferred_element_type=F32)
    for r in range(1, kept):
        total += jnp.dot(tile_buf[r], int_buf[block_of[r]], preferred_element_type=F32)
    out_ref[...] = total

    for d in range(planes):
        amp_y(d).wait_send()
        if d > 0:
            both_sides(d, lambda to, _: amp_z(z, to).wait_send())
    for p in range(pieces):
        for d in range(chips):
            int_c(d, p).wait_send()
            if d > 0:
                int_x(d, p).wait_send()


def solution(mesh):
    n_blk, n_grp = mesh.shape["blk"], mesh.shape["grp"]

    def on_device(amps, domains, owner, coupling, integrals):
        slots, width, depth = amps.shape
        cols = integrals.shape[1]
        group = slots * n_grp
        pieces = 4
        chips, planes = n_blk // 2, n_grp // 2
        dma = pltpu.SemaphoreType.DMA
        vmem = pl.BlockSpec(memory_space=pltpu.VMEM)
        return pl.pallas_call(
            functools.partial(kernel, n_blk, n_grp, pieces),
            out_shape=jax.ShapeDtypeStruct((group, cols), F32),
            in_specs=[pl.BlockSpec(memory_space=pltpu.HBM)] * 5,
            out_specs=vmem,
            scratch_shapes=[
                pltpu.VMEM(amps.shape, BF16),
                pltpu.VMEM((width, domains.shape[0]), jnp.int32),
                pltpu.VMEM((1, owner.shape[0]), jnp.int32),
                pltpu.SMEM(coupling.shape, jnp.int32),
                dma((4,)),
                pltpu.VMEM((group * width, depth), BF16),
                pltpu.VMEM((n_blk, depth, cols), BF16),
                pltpu.VMEM((n_blk // 2, group, depth), BF16),
                pltpu.VMEM((group, group * width), F32),
                dma((planes,)), dma((planes,)), dma((planes,)), dma((planes,)),
                dma((chips, pieces)), dma((chips, pieces)), dma((chips, pieces)), dma((chips, pieces)),
                dma(()), pltpu.SemaphoreType.REGULAR((planes,)),
            ],
            compiler_params=pltpu.CompilerParams(
                collective_id=0, has_side_effects=True, vmem_limit_bytes=48 * 1024 * 1024),
        )(*(pltpu.with_memory_space_constraint(a, pltpu.HBM) for a in (amps, domains.T, owner.reshape(1, -1), coupling, integrals)))

    return jax.shard_map(
        on_device,
        mesh=mesh,
        in_specs=(P(("blk", "grp"), None, None), P(), P(), P(), P("blk", "grp")),
        out_specs=P("blk", "grp"),
        check_vma=False,
    )
```

```python
import functools

import jax
import jax.numpy as jnp
from jax import lax
from jax.experimental import pallas as pl
from jax.experimental.pallas import tpu as pltpu
from jax.sharding import PartitionSpec as P

MESH = pl.DeviceIdType.MESH
F32 = jnp.float32
BF16 = jnp.bfloat16


def kernel(
    n_blk, n_grp, pieces,
    amps_hbm, dom_hbm, owner_hbm, coupling_hbm, ints_ref, out_ref,
    amps_ref, dom_ref, owner_ref, coupling_ref, load_sem, amp_buf, int_buf, tile_buf, code_buf,
    amp_z_send, amp_z_recv, amp_y_send, amp_y_recv,
    int_x_send, int_x_recv, int_c_send, int_c_recv, local_sem, ready,
):
    chips, planes = n_blk // 2, n_grp // 2
    blk, grp = lax.axis_index("blk"), lax.axis_index("grp")
    x, core = blk // 2, blk % 2
    z, y = grp // 2, grp % 2
    slots, width, depth = amps_ref.shape
    rows = slots * width
    cols = ints_ref.shape[1]
    group = slots * n_grp
    nvb = n_blk
    target = grp // (depth // cols)
    cut = depth // pieces

    def at(b, g):
        return (b, g)

    barrier = pltpu.get_barrier_semaphore()

    def greet(b, g):
        pl.semaphore_signal(barrier, inc=1, device_id=at(b, g), device_id_type=MESH)

    for d in range(1, chips):
        greet(((x + d) % chips) * 2 + core, grp)
    greet(x * 2 + 1 - core, grp)
    greet(blk, z * 2 + 1 - y)
    pl.when(z > 0)(lambda: greet(blk, grp - 2))
    pl.when(z < planes - 1)(lambda: greet(blk, grp + 2))

    loads = [
        pltpu.make_async_copy(src, dst, load_sem.at[i])
        for i, (src, dst) in enumerate((
            (amps_hbm, amps_ref), (dom_hbm, dom_ref), (owner_hbm, owner_ref), (coupling_hbm, coupling_ref)))
    ]
    for load in loads:
        load.start()
    own_copy = pltpu.make_async_copy(ints_ref, int_buf.at[blk], local_sem)
    own_copy.start()
    at_edge = jnp.where((z == 0) | (z == planes - 1), 1, 0)
    pl.semaphore_wait(barrier, chips + 3 - at_edge)

    def amp_rows(g):
        return amp_buf.at[pl.ds(pl.multiple_of(g * rows, rows), rows)]

    def int_rows(b, p):
        return int_buf.at[b, pl.ds(p * cut, cut)]

    def amp_z(src, dst):
        return pltpu.make_async_remote_copy(
            src_ref=amp_rows(src * 2 + y), dst_ref=amp_rows(src * 2 + y),
            send_sem=amp_z_send.at[dst], recv_sem=amp_z_recv.at[src],
            device_id=at(blk, dst * 2 + y), device_id_type=MESH)

    def amp_y(src):
        return pltpu.make_async_remote_copy(
            src_ref=amp_rows(src * 2 + y), dst_ref=amp_rows(src * 2 + y),
            send_sem=amp_y_send.at[src], recv_sem=amp_y_recv.at[src],
            device_id=at(blk, z * 2 + 1 - y), device_id_type=MESH)

    def both_sides(d, do):
        pl.when(z >= d)(lambda: do(z - d, 1))
        pl.when(z < planes - d)(lambda: do(z + d, -1))

    def int_x(d, p):
        return pltpu.make_async_remote_copy(
            src_ref=ints_ref.at[pl.ds(p * cut, cut)], dst_ref=int_rows(blk, p),
            send_sem=int_x_send.at[d, p], recv_sem=int_x_recv.at[d, p],
            device_id=at(((x + d) % chips) * 2 + core, grp), device_id_type=MESH)

    def int_c(d, p):
        b = ((x + chips - d) % chips) * 2 + core
        src = ints_ref.at[pl.ds(p * cut, cut)] if d == 0 else int_rows(b, p)
        return pltpu.make_async_remote_copy(
            src_ref=src, dst_ref=int_rows(b, p),
            send_sem=int_c_send.at[d, p], recv_sem=int_c_recv.at[d, p],
            device_id=at(x * 2 + 1 - core, grp), device_id_type=MESH)

    for p in range(pieces):
        for d in range(1, chips):
            int_x(d, p).start()
    def tell(other, step):
        def say():
            pl.semaphore_signal(ready.at[other], inc=1, device_id=at(blk, (z + step) * 2 + y), device_id_type=MESH)
        pl.when((z + step >= 0) & (z + step < planes))(say)

    def heard(other, step):
        pl.semaphore_wait(ready.at[other], 1)
        tell(other, step)
        amp_z(z, other).start()

    both_sides(1, tell)
    loads[0].wait()
    amp_rows(grp)[...] = amps_ref[...].astype(F32).reshape(rows, depth).astype(BF16)
    both_sides(1, lambda to, _: amp_z(z, to).start())
    amp_y(z).start()

    for p in range(pieces):
        int_c(0, p).start()

    for load in loads[1:]:
        load.wait()
    dom = dom_ref[:, pl.ds(pl.multiple_of(blk * group, group), group)]
    own = owner_ref[:, pl.ds(pl.multiple_of(blk * group, group), group)] - blk * group
    hit = jnp.max((dom == target).astype(F32), axis=0, keepdims=True)
    keep = jnp.zeros(dom.shape, F32)
    kept = nvb // 2
    rank = jnp.int32(0)
    block_of = [jnp.int32(0)] * kept
    for c in range(nvb):
        on = (coupling_ref[c, target] > 0).astype(jnp.int32)
        for r in range(kept):
            block_of[r] += jnp.where((on > 0) & (rank == r), c, 0)
        rank += on
        keep = jnp.where(dom == c, (on * rank).astype(F32), keep)
    code = keep * hit
    j_slot = lax.broadcasted_iota(jnp.int32, (group, group * width), 1) // width
    spread = (j_slot == lax.broadcasted_iota(jnp.int32, (group, group * width), 0)).astype(F32)
    by_row = jnp.dot(code.astype(BF16), spread.astype(BF16), preferred_element_type=F32)
    j_k = lax.broadcasted_iota(jnp.int32, (width, group * width), 1) % width
    pick = j_k == lax.broadcasted_iota(jnp.int32, (width, group * width), 0)
    code_row = jnp.sum(jnp.where(pick, by_row, 0.0), axis=0, keepdims=True)
    diag = lax.broadcasted_iota(jnp.int32, (group, group), 0) == lax.broadcasted_iota(
        jnp.int32, (group, group), 1)
    own_col = jnp.sum(jnp.where(diag, own.astype(F32), 0.0), axis=1, keepdims=True)
    code_buf[...] = jnp.where(own_col == j_slot.astype(F32), code_row, 0.0)

    arrivals = [(d, p) for p in range(pieces) for d in range(1, chips)]

    def pass_int(some):
        for d, p in some:
            int_x(d, p).wait_recv()
            int_c(d, p).start()

    def pass_amp(src, _):
        amp_z(src, z).wait_recv()
        amp_y(src).start()

    for d in range(2, planes):
        both_sides(d, heard)
        both_sides(d - 1, pass_amp)
    pass_int(arrivals)
    both_sides(planes - 1, pass_amp)
    for src in range(planes):
        amp_y(src).wait_recv()

    def build(c, _):
        sel = (code_buf[...] == (c + 1).astype(F32)).astype(F32).astype(BF16)
        tile_buf[c] = jnp.dot(sel, amp_buf[...], preferred_element_type=F32).astype(BF16)
        return 0

    if kept <= 4:
        for r in range(kept):
            build(jnp.int32(r), 0)
    else:
        lax.fori_loop(0, kept, build, 0)

    own_copy.wait()
    for p in range(pieces):
        for d in range(chips):
            int_c(d, p).wait_recv()
    total = jnp.dot(tile_buf[0], int_buf[block_of[0]], preferred_element_type=F32)
    for r in range(1, kept):
        total += jnp.dot(tile_buf[r], int_buf[block_of[r]], preferred_element_type=F32)
    out_ref[...] = total

    for d in range(planes):
        amp_y(d).wait_send()
        if d > 0:
            both_sides(d, lambda to, _: amp_z(z, to).wait_send())
    for p in range(pieces):
        for d in range(chips):
            int_c(d, p).wait_send()
            if d > 0:
                int_x(d, p).wait_send()


def solution(mesh):
    n_blk, n_grp = mesh.shape["blk"], mesh.shape["grp"]

    def on_device(amps, domains, owner, coupling, integrals):
        slots, width, depth = amps.shape
        cols = integrals.shape[1]
        group = slots * n_grp
        pieces = 4
        chips, planes = n_blk // 2, n_grp // 2
        dma = pltpu.SemaphoreType.DMA
        vmem = pl.BlockSpec(memory_space=pltpu.VMEM)
        return pl.pallas_call(
            functools.partial(kernel, n_blk, n_grp, pieces),
            out_shape=jax.ShapeDtypeStruct((group, cols), F32),
            in_specs=[pl.BlockSpec(memory_space=pltpu.HBM)] * 5,
            out_specs=vmem,
            scratch_shapes=[
                pltpu.VMEM(amps.shape, BF16),
                pltpu.VMEM((width, domains.shape[0]), jnp.int32),
                pltpu.VMEM((1, owner.shape[0]), jnp.int32),
                pltpu.SMEM(coupling.shape, jnp.int32),
                dma((4,)),
                pltpu.VMEM((group * width, depth), BF16),
                pltpu.VMEM((n_blk, depth, cols), BF16),
                pltpu.VMEM((n_blk // 2, group, depth), BF16),
                pltpu.VMEM((group, group * width), F32),
                dma((planes,)), dma((planes,)), dma((planes,)), dma((planes,)),
                dma((chips, pieces)), dma((chips, pieces)), dma((chips, pieces)), dma((chips, pieces)),
                dma(()), pltpu.SemaphoreType.REGULAR((planes,)),
            ],
            compiler_params=pltpu.CompilerParams(
                collective_id=0, has_side_effects=True, vmem_limit_bytes=48 * 1024 * 1024),
        )(*(pltpu.with_memory_space_constraint(a, pltpu.HBM) for a in (amps, domains.T, owner.reshape(1, -1), coupling, integrals)))

    return jax.shard_map(
        on_device,
        mesh=mesh,
        in_specs=(P(("blk", "grp"), None, None), P(), P(), P(), P("blk", "grp")),
        out_specs=P("blk", "grp"),
        check_vma=False,
    )
```
